32 devices in a mesh: groups: 2 (over x), tiles: 16 (over z, y, core).
Axes of the slice: x: 2, y: 2, z: 4, core: 2. Of those that a mesh axis runs over, the one named last changes fastest.
Arguments:
- control: float32 [6, 64, 256, 128], P('groups', None, 'tiles'), parts along dimension 0, may hold values from -6 to 6
- departures: float32 [2048, 768], P(('groups', 'tiles')), parts along dimension 0, may hold values from -6 to 6
- obs_cell: int32 [2048], P(('groups', 'tiles')), parts along dimension 0, may hold values from 0 to 2047
- obs_owner: int32 [2048, 1], P(('groups', 'tiles')), parts along dimension 0, may hold values from 0 to 15; in each aligned block of 64 rows (0 to 63, 64 to 127, ...) at most 8 rows name the same one
- scale_class: int32 [256, 128], P('tiles'), may hold values from 0 to 7
- sea_mask: int32 [256, 128], P('tiles'), may hold values 0 or 1
- class_table: float32 [2, 8], replicated, may hold values from 0.02 to 0.24
- obs_precision: float32 [3072, 192], P('tiles'), as said below
Outputs:
- increment: float32 [6, 64, 256, 128], P('groups', None, 'tiles'), parts along dimension 0
- gradient: float32 [6, 64, 256, 128], P('groups', None, 'tiles'), parts along dimension 0
The draws below stay inside these ranges and needn't reach their ends.
There are 2 independent parts, one for each index of `groups`. The reference program is written for one: setup_inputs(seed, part) draws one part's arguments, and reference() takes and returns one part's arrays. A program takes and returns all parts, laid end to end along the dimension named above; an argument that names none is the same for every part. Nothing has to cross between parts.
Inputs may be any that keep to these rules, and one draw needn't show every extreme that they name: `obs_owner`: among the profiles of one tile no owner is named more than 8 times; some owner exactly 8 times. `obs_precision`: each owner's block is symmetric and positive definite.
All inputs are finite; a program needn't handle non-finite values. No bound on the sum of `sea_mask` on one device may be relied on, other than what follows from the above.
Results may differ from the reference program's by a relative error of at most 0.00015.
Values sent between devices are 32-bit elements; how exact they have to be, the bound alone decides.
A program may use at most 64 MiB of HBM per device.

```python
import math
import jax
import jax.numpy as jnp
import numpy as np
from jax import lax

FIELDS = 3
LEV = 64
CX = 16
NY = 128
STEPS = 8
MEMBERS = 4
NCLASS = 8
OBS_DEV = 64
CH = 192
NX = 256
PROFILES = 1024
CAP = 8
PREC_ROWS = 3072
N_TILES = 16


def draw_obs_precision(key, part):
    key = jax.random.fold_in(key, 11)
    key_off, key_diag, key_scale = jax.random.split(key, 3)
    owners = PREC_ROWS // CH
    raw = jax.random.uniform(key_off, (owners, CH, CH), jnp.float32, -1.0, 1.0)
    symmetric = 0.5 * (raw + jnp.transpose(raw, (0, 2, 1)))
    identity = jnp.eye(CH, dtype=jnp.float32)
    diagonal = CH - 1 + jax.random.uniform(key_diag, (owners, CH, 1), jnp.float32, 0.5, 1.5)
    factor = jnp.exp(jax.random.uniform(key_scale, (owners, 1, 1), jnp.float32, math.log(0.5), math.log(2.0)))
    matrix = (symmetric * (1.0 - identity) + identity * diagonal) * factor / (CH - 1)
    return matrix.reshape(PREC_ROWS, CH).astype(jnp.float32)


def set_ends(array, key, smallest, high):
    place = [jax.random.randint(jax.random.fold_in(key, axis), (), 0, length) for axis, length in enumerate(array.shape)]
    widest = array.shape.index(max(array.shape))
    beside = place[:widest] + [(place[widest] + 1) % array.shape[widest]] + place[widest + 1:]
    return array.at[tuple(place)].set(smallest).at[tuple(beside)].set(high)


def shard_levels(key, dims, cuts, least, high):
    loudness = 1.0
    for position, shards_of in cuts:
        heights = jax.random.uniform(jax.random.fold_in(jax.random.fold_in(key, 6), position), (shards_of,), jnp.float32, least / len(cuts), high / len(cuts))
        loudness = loudness * jnp.repeat(jnp.exp(heights), dims[position] // shards_of).reshape((-1,) + (1,) * (len(dims) - 1 - position))
    return loudness


def deal_out(own_key, own, number, rows, number_of, top, limit, skew):
    sequence = jax.random.permutation(own_key, number_of)
    heavy_load, common = shares(number_of, rows * top, limit, skew, True), shares(number_of, rows * top, limit, skew, False)
    places = jnp.arange(number_of)

    def named(tallies, rotation):
        used = int((tallies > 0).sum())
        fixed = max(1, used // 4)
        passed = fixed + (places - fixed + rotation * (used - fixed)) % max(1, number_of - fixed)
        return jnp.zeros((number_of,), jnp.int32).at[sequence[jnp.where(places < fixed, places, passed)]].set(jnp.asarray(tallies, jnp.int32))

    tallies = jnp.where(number % 4 == 0, named(heavy_load, number // 4), named(common, number - number // 4 - 1))
    mixed = jax.random.permutation(jax.random.fold_in(own, 3), number_of)
    giver, sink = mixed[0:number_of // 2 * 2:2], mixed[1:number_of // 2 * 2:2]
    slack = jnp.minimum(tallies[giver] - 1, limit - tallies[sink]) // 2
    slack = jnp.where((giver == sequence[0]) | (sink == sequence[0]) | (tallies[sink] == 0), 0, jnp.maximum(slack, 0))
    passed = jax.random.randint(jax.random.fold_in(own, 4), (number_of // 2,), 0, 1 << 20) % (slack + 1)
    tallies = tallies.at[giver].add(-passed).at[sink].add(passed)
    labels = jnp.searchsorted(jnp.cumsum(tallies), jnp.arange(rows * top), side="right").astype(jnp.int32)
    listing = labels.reshape(top, rows).T
    listing = listing[jax.random.permutation(jax.random.fold_in(own, 1), rows)]
    rotation = jax.random.randint(jax.random.fold_in(own, 2), (rows, 1), 0, top)
    return jnp.take_along_axis(listing, (jnp.arange(top)[None, :] + rotation) % top, axis=1)


def shares(count, total, reach, slope, full):
    portions = [(1 << 20) // math.isqrt(standing ** slope) + 1 for standing in range(1, count + 1)]
    largest = reach if full else min(reach, max(-(-total // count), total * portions[0] // sum(portions)))
    least = 1 if total - largest >= count - 1 else 0
    counts, rest = [largest] + [least] * (count - 1), total - largest - least * (count - 1)
    while rest > 0:
        movable = [i for i in range(1, count) if counts[i] < largest] or [i for i in range(1, count) if counts[i] < reach]
        pool, remaining = sum([portions[i] for i in movable]), rest
        for i in movable:
            more = min(reach - counts[i], max(1, remaining * portions[i] // pool), rest)
            counts[i] = counts[i] + more
            rest = rest - more
    return np.array(counts)


def bell_draw(stream_key, dims, width, limit, cuts=(), kind=jnp.bfloat16):
    array = width * jax.random.normal(stream_key, dims, jnp.float32)
    if cuts:
        array = array * shard_levels(stream_key, dims, cuts, -0.22, 0.18)
    return jnp.clip(array, -limit, limit).astype(kind)


def setup_inputs(seed: int = 0, part: int = 0) -> dict:
    seeds = jax.random.split(jax.random.key(seed), 9)
    own_keys = jax.random.split(jax.random.fold_in(seeds[8], part), 9)
    control = bell_draw(own_keys[0], (FIELDS, LEV, NX, NY), 1.0, 6.0, ((2, 16),), jnp.float32)
    departures = bell_draw(own_keys[1], (PROFILES, MEMBERS * CH), 1.0, 6.0, ((0, 16),), jnp.float32)
    obs_cell = set_ends(jax.random.randint(own_keys[2], (PROFILES,), 0, CX * NY), jax.random.fold_in(own_keys[2], 1), 0, (CX * NY) - 1).astype(jnp.int32)
    obs_owner_keys = jax.random.split(jax.random.fold_in(own_keys[3], 1), PROFILES // OBS_DEV)
    obs_owner_turns = jax.random.permutation(jax.random.fold_in(own_keys[3], 3), PROFILES // OBS_DEV)
    obs_owner = jax.vmap(lambda own, number: deal_out(jax.random.fold_in(own_keys[3], 2), own, number, OBS_DEV, N_TILES, 1, CAP, 2))(obs_owner_keys, obs_owner_turns).reshape((PROFILES, 1))
    scale_class = set_ends(jax.random.randint(seeds[4], (NX, NY), 0, NCLASS), jax.random.fold_in(seeds[4], 1), 0, NCLASS - 1).astype(jnp.int32)
    sea_mask = set_ends((jax.random.randint(seeds[5], (NX, NY), 0, 8) < 7).astype(jnp.int32), jax.random.fold_in(seeds[5], 1), 0, 1)
    class_table = jnp.clip(jnp.exp(jax.random.uniform(seeds[6], (2, NCLASS), jnp.float32, math.log(0.02), math.log(0.24))), 0.02, 0.24)
    obs_precision = draw_obs_precision(jax.random.fold_in(seeds[8], 71), part)
    return dict(control=control, departures=departures, obs_cell=obs_cell, obs_owner=obs_owner, scale_class=scale_class, sea_mask=sea_mask, class_table=class_table, obs_precision=obs_precision)


def face_fields(scale_class, sea_mask, class_table):
    classes = jnp.arange(NCLASS, dtype=jnp.int32)
    selector = (scale_class[None] == classes[:, None, None]).astype(jnp.float32)
    kappa_x = jnp.sum(selector * class_table[0][:, None, None], axis=0)
    kappa_y = jnp.sum(selector * class_table[1][:, None, None], axis=0)
    ocean = sea_mask.astype(jnp.float32)
    face_x = 0.5 * (kappa_x + jnp.roll(kappa_x, -1, 0)) * ocean * jnp.roll(ocean, -1, 0)
    face_y = 0.5 * (kappa_y[:, :-1] + kappa_y[:, 1:]) * ocean[:, :-1] * ocean[:, 1:]
    return ocean, face_x, face_y


def diffuse_full(state, face_x, face_y):
    for step_index in range(STEPS):
        flux_x = face_x * (jnp.roll(state, -1, 2) - state)
        change = flux_x - jnp.roll(flux_x, 1, 2)
        flux_y = face_y * (state[..., 1:] - state[..., :-1])
        zeros = jnp.zeros(state.shape[:-1] + (1,), jnp.float32)
        change = change + jnp.concatenate([flux_y, zeros], axis=-1) - jnp.concatenate([zeros, flux_y], axis=-1)
        state = state + change
    return state


def owner_apply(blocks):
    misfit_block, owner_block, tiles_all = blocks
    chosen = tiles_all[owner_block]
    weighted = jnp.einsum("pmc,pcd->pmd", misfit_block, chosen, precision=lax.Precision.HIGHEST)
    energy = jnp.sum(misfit_block * weighted, axis=-1, keepdims=True) / CH
    return weighted / (1.0 + energy)


def reference(control, departures, obs_cell, obs_owner, scale_class, sea_mask, class_table, obs_precision):
    ocean, face_x, face_y = face_fields(scale_class, sea_mask, class_table)
    increment = diffuse_full(ocean * control, face_x, face_y)
    profile_count = obs_cell.shape[0]
    tile_of = jnp.arange(profile_count, dtype=jnp.int32) // OBS_DEV
    grid_x = (tile_of * CX + obs_cell // NY).astype(jnp.int32)
    grid_y = (obs_cell % NY).astype(jnp.int32)
    seen = increment[:, :, grid_x, grid_y]
    model_eq = seen.reshape(CH, profile_count).T
    misfit = model_eq[:, None, :] - departures.reshape(profile_count, MEMBERS, CH)
    tiles_all = obs_precision.reshape(N_TILES, CH, CH)
    misfit_tiles = misfit.reshape(N_TILES, OBS_DEV, MEMBERS, CH)
    owner_tiles = obs_owner[:, 0].reshape(N_TILES, OBS_DEV)
    obs_grad = lax.map(lambda pair: owner_apply((pair[0], pair[1], tiles_all)), (misfit_tiles, owner_tiles))
    summed = jnp.sum(obs_grad.reshape(profile_count, MEMBERS, CH), axis=1)
    adjoint = jnp.zeros(control.shape, jnp.float32)
    adjoint = adjoint.at[:, :, grid_x, grid_y].add(summed.T.reshape(FIELDS, LEV, profile_count))
    gradient = control + ocean * diffuse_full(adjoint, face_x, face_y)
    return increment, gradient
```

```python
import functools
import jax
import jax.numpy as jnp
from jax import lax
from jax.experimental import pallas as pl
from jax.experimental.pallas import tpu as pltpu
from jax.sharding import PartitionSpec as P

STEPS = 8
MEMBERS = 4
CHUNKS = 6
HIGHEST = lax.Precision.HIGHEST
F32 = jnp.float32
BF16 = jnp.bfloat16
I32 = jnp.int32


def sweep(load_row, fx_ref, fy_ref, emit, rows):
    current = [None] * (STEPS + 1)
    flux = [None] * (STEPS + 1)
    for i in range(rows):
        value = load_row(i)
        for s in range(1, STEPS + 1):
            before, current[s] = current[s], value
            if before is None:
                break
            r = i - s
            flux_x = fx_ref[r] * (value - before)
            last, flux[s] = flux[s], flux_x
            if last is None:
                break
            flux_y = fy_ref[r] * (pltpu.roll(before, before.shape[1] - 1, 1) - before)
            value = before + ((flux_x - last) + (flux_y - pltpu.roll(flux_y, 1, 1)))
        else:
            emit(i - STEPS, value)


def split(x):
    high = x.astype(BF16)
    return high, (x - high.astype(F32)).astype(BF16)


def observe_kernel(
    tiles, cap, chan, cx,
    table, control, departures, cell_ref, owner_ref, class_ref, mask_ref, precision_ref,
    inc_out, back_out, cells_out, fxb, fyb, ocb,
    own, halo_l, halo_r, inc, geo, geo_l, geo_r, cells, cells_in, hot, model_t,
    dep_send, dep_recv, mod_send, mod_recv, ans, back, weighted_dep,
    local_sem, out_sem, back_sem, halo_send, halo_recv, geo_send, geo_recv, a2a_send, a2a_recv,
):
    me = lax.axis_index("tiles")
    h = STEPS
    ext = cx + 2 * h
    slots = tiles * cap
    nc = chan // CHUNKS
    ny = own.shape[2]
    right = lax.rem(me + 1, tiles)
    left = lax.rem(me + tiles - 1, tiles)

    own_copy = pltpu.make_async_copy(control, own, local_sem)
    own_copy.start()
    geo[0] = class_ref[...]
    geo[1] = mask_ref[...]

    barrier = pltpu.get_barrier_semaphore()

    @pl.loop(1, tiles)
    def _(k):
        pl.semaphore_signal(barrier, inc=1, device_id={"tiles": lax.rem(me + k, tiles)}, device_id_type=pl.DeviceIdType.MESH)

    pl.semaphore_wait(barrier, tiles - 1)

    def remote(src, dst, send, recv, to):
        return pltpu.make_async_remote_copy(
            src_ref=src, dst_ref=dst, send_sem=send, recv_sem=recv,
            device_id={"tiles": to}, device_id_type=pl.DeviceIdType.MESH,
        )

    geo_copies = [
        remote(geo.at[:, pl.ds(cx - h, h)], geo_l, geo_send.at[0], geo_recv.at[0], right),
        remote(geo.at[:, pl.ds(0, h)], geo_r, geo_send.at[1], geo_recv.at[1], left),
    ]
    for copy in geo_copies:
        copy.start()
    halo_copies = []
    for q in range(CHUNKS):
        part = pl.ds(q * nc, nc)
        pair = [
            remote(control.at[part, pl.ds(cx - h, h)], halo_l.at[part], halo_send.at[0, q], halo_recv.at[0, q], right),
            remote(control.at[part, pl.ds(0, h)], halo_r.at[part], halo_send.at[1, q], halo_recv.at[1, q], left),
        ]
        for copy in pair:
            copy.start()
        halo_copies.append(pair)

    n = departures.shape[0]
    eye = lax.broadcasted_iota(I32, (n, n), 0) == lax.broadcasted_iota(I32, (n, n), 1)
    lower = lax.broadcasted_iota(I32, (n, n), 1) < lax.broadcasted_iota(I32, (n, n), 0)
    owner_row = owner_ref[...]
    owner_col = jnp.sum(jnp.where(eye, owner_row, 0), axis=1, keepdims=True)
    cell_col = jnp.sum(jnp.where(eye, cell_ref[...], 0), axis=1, keepdims=True)
    slot_col = jnp.sum(jnp.where((owner_col == owner_row) & lower, 1, 0), axis=1, keepdims=True)
    offset = owner_col - me
    offset = jnp.where(offset < 0, offset + tiles, offset)
    dest_col = offset * cap + slot_col
    dest_row = jnp.sum(jnp.where(eye, dest_col, 0), axis=0, keepdims=True)
    place = jnp.where(lax.broadcasted_iota(I32, (slots, n), 0) == dest_row, 1.0, 0.0).astype(F32)
    spread = jnp.dot(place, departures[...], precision=HIGHEST, preferred_element_type=F32)
    dep_send[...] = spread.reshape(dep_send.shape)

    def exchange(src_of, dst, phase):
        @pl.loop(1, tiles)
        def _(k):
            src, to = src_of(k)
            remote(src, dst.at[k], a2a_send.at[phase], a2a_recv.at[phase], to).start()

    def landed(buffer, sem):
        pltpu.make_async_copy(buffer.at[pl.ds(1, tiles - 1)], buffer.at[pl.ds(1, tiles - 1)], sem).wait()

    exchange(lambda k: (dep_send.at[k], lax.rem(me + k, tiles)), dep_recv, 0)
    dep_recv[0] = dep_send[0]

    slot_lane = lax.broadcasted_iota(I32, (n, slots), 1)

    def cell_row(dest):
        return jnp.sum(jnp.where(dest == slot_lane, cell_col + 1, 0), axis=0, keepdims=True) - 1

    later = jnp.where(offset + 1 == tiles, 0, offset + 1) * cap + slot_col
    sooner = jnp.where(offset == 0, tiles - 1, offset - 1) * cap + slot_col
    mine = cell_row(dest_col)
    for j, row in enumerate((cell_row(later), mine, cell_row(sooner))):
        cells[j] = jnp.broadcast_to(row, cells.shape[1:])
    cell_copies = [
        remote(cells.at[0], cells_in.at[0], geo_send.at[2], geo_recv.at[2], left),
        remote(cells.at[2], cells_in.at[1], geo_send.at[3], geo_recv.at[3], right),
    ]
    for copy in cell_copies:
        copy.start()
    for j in range(cx // 2):
        index = lax.broadcasted_iota(I32, (2 * ny, slots), 0) + 2 * j * ny
        hot[j] = jnp.where(index == mine, 1.0, 0.0).astype(BF16)

    for copy in geo_copies:
        copy.wait()
    kinds = jnp.concatenate([geo_l[0], geo[0], geo_r[0]], axis=0)
    ocean = jnp.concatenate([geo_l[1], geo[1], geo_r[1]], axis=0).astype(F32)
    kx = jnp.zeros((ext, ny), F32)
    ky = jnp.zeros((ext, ny), F32)
    for c in range(table.shape[1]):
        kx = jnp.where(kinds == c, table[0, c], kx)
        ky = jnp.where(kinds == c, table[1, c], ky)
    face_x = 0.5 * (kx + pltpu.roll(kx, ext - 1, 0)) * ocean * pltpu.roll(ocean, ext - 1, 0)
    face_y = 0.5 * (ky + pltpu.roll(ky, ny - 1, 1)) * ocean * pltpu.roll(ocean, ny - 1, 1)
    face_y = jnp.where(lax.broadcasted_iota(I32, (ext, ny), 1) < ny - 1, face_y, 0.0)
    for r in range(ext):
        fxb[r] = jnp.broadcast_to(face_x[r : r + 1], (8, ny))
        fyb[r] = jnp.broadcast_to(face_y[r : r + 1], (8, ny))
        ocb[r] = jnp.broadcast_to(ocean[r : r + 1], (8, ny))

    own_copy.wait()
    own2, left2, right2, inc2 = (
        own.reshape(chan * cx, ny), halo_l.reshape(chan * h, ny), halo_r.reshape(chan * h, ny), inc.reshape(chan * cx, ny)
    )
    inc_copies = []
    for q in range(CHUNKS):
        for copy in halo_copies[q]:
            copy.wait_recv()

        @pl.loop(q * nc // 8, (q + 1) * nc // 8)
        def _(g):
            def load_row(i):
                if i < h:
                    row = left2[pl.ds(g * 8 * h + i, 8, stride=h), :]
                elif i < h + cx:
                    row = own2[pl.ds(g * 8 * cx + i - h, 8, stride=cx), :]
                else:
                    row = right2[pl.ds(g * 8 * h + i - h - cx, 8, stride=h), :]
                return ocb[i] * row

            def emit(r, value):
                inc2[pl.ds(g * 8 * cx + r - h, 8, stride=cx), :] = value

            sweep(load_row, fxb, fyb, emit, ext)

        part = pl.ds(q * nc, nc)
        copy = pltpu.make_async_copy(inc.at[part], inc_out.at[part], out_sem.at[q])
        copy.start()
        inc_copies.append(copy)
        total = jnp.zeros((nc, slots), F32)
        for j in range(cx // 2):
            pair = jnp.concatenate(
                [inc2[pl.ds(q * nc * cx + 2 * j + b, nc, stride=cx), :] for b in range(2)], axis=1
            )
            for piece in split(pair):
                total += jnp.dot(piece, hot[j], preferred_element_type=F32)
        model_t[part] = total

    mod_send[...] = model_t[...].T.reshape(mod_send.shape)
    exchange(lambda k: (mod_send.at[k], lax.rem(me + k, tiles)), mod_recv, 1)
    mod_recv[0] = mod_send[0]
    precision = precision_ref[...]
    landed(dep_recv, a2a_recv.at[0])
    for m in range(MEMBERS):
        rows = dep_recv[:, :, m * chan : (m + 1) * chan].reshape(slots, chan)
        weighted_dep[m] = jnp.dot(rows, precision, precision=HIGHEST, preferred_element_type=F32)
    landed(mod_recv, a2a_recv.at[1])
    model = mod_recv[...].reshape(slots, chan)
    weighted_model = jnp.dot(model, precision, precision=HIGHEST, preferred_element_type=F32)
    answer = jnp.zeros((slots, chan), F32)
    for m in range(MEMBERS):
        misfit = model - dep_recv[:, :, m * chan : (m + 1) * chan].reshape(slots, chan)
        weighted = weighted_model - weighted_dep[m]
        energy = jnp.sum(misfit * weighted, axis=1, keepdims=True) / chan
        answer += weighted / (1.0 + energy)
    answer = answer.reshape(tiles, cap, chan)
    ans[pl.ds(1, tiles)] = answer
    ans[0] = answer[tiles - 1]
    ans[tiles + 1] = answer[0]
    exchange(lambda k: (ans.at[pl.ds(k, 3)], lax.rem(me - k + tiles, tiles)), back, 2)
    for j in range(3):
        back[0, j] = ans[j]
    for copy in cell_copies:
        copy.wait()
    cells_out[0] = cells_in[0]
    cells_out[1] = cells[1]
    cells_out[2] = cells_in[1]
    for pair in halo_copies:
        for copy in pair:
            copy.wait_send()
    landed(dep_recv, a2a_send.at[0])
    landed(mod_recv, a2a_send.at[1])
    for copy in inc_copies:
        copy.wait()
    landed(back, a2a_recv.at[2])
    landed(back, a2a_send.at[2])
    copy = pltpu.make_async_copy(back, back_out, back_sem)
    copy.start()
    copy.wait()


def adjoint_kernel(
    chan, cx,
    control, inc_in, back, cells, fxb, fyb, ocb,
    inc_out, grad_out,
    own, field, grad, inc_sem, own_sem, out_sem,
):
    h = STEPS
    ext = cx + 2 * h
    ny = own.shape[2]
    nc = chan // CHUNKS
    tiles, _, cap, _ = back.shape
    slots = tiles * cap
    own_copy = pltpu.make_async_copy(control, own, own_sem)
    own_copy.start()
    inc_copy = pltpu.make_async_copy(inc_in, inc_out, inc_sem)
    inc_copy.start()
    eye = lax.broadcasted_iota(I32, (slots, slots), 0) == lax.broadcasted_iota(I32, (slots, slots), 1)
    for j, start, first, count in ((1, h, 0, cx), (0, h + cx, 0, h), (2, 0, cx - h, h)):
        rows_t = back[:, j].reshape(slots, chan).T
        lhs = jnp.concatenate(split(rows_t), axis=1)
        cell = jnp.sum(jnp.where(eye, cells[j, 0:1], 0), axis=1, keepdims=True)
        for x in range(0, count, 2):
            index = lax.broadcasted_iota(I32, (slots, 2 * ny), 1) + (first + x) * ny
            hot = jnp.where(index == cell, 1.0, 0.0).astype(BF16)
            out = jnp.dot(lhs, jnp.concatenate([hot, hot], axis=0), preferred_element_type=F32)
            field[start + x] = out[:, :ny]
            field[start + x + 1] = out[:, ny:]
    own_copy.wait()
    own2, grad2 = own.reshape(chan * cx, ny), grad.reshape(chan * cx, ny)
    copies = []
    for q in range(CHUNKS):

        @pl.loop(q * nc // 8, (q + 1) * nc // 8)
        def _(g):
            def load_row(i):
                return field[i, pl.ds(pl.multiple_of(g * 8, 8), 8), :]

            def emit(r, value):
                at = pl.ds(g * 8 * cx + r - h, 8, stride=cx)
                grad2[at, :] = own2[at, :] + ocb[r] * value

            sweep(load_row, fxb, fyb, emit, ext)

        part = pl.ds(q * nc, nc)
        copy = pltpu.make_async_copy(grad.at[part], grad_out.at[part], out_sem.at[q])
        copy.start()
        copies.append(copy)
    for copy in copies:
        copy.wait()
    inc_copy.wait()


def body(control, departures, obs_cell, obs_owner, scale_class, sea_mask, class_table, obs_precision):
    fields, levels, cx, ny = control.shape
    chan = fields * levels
    n = obs_cell.shape[0]
    tiles = lax.axis_size("tiles")
    cap = -(-max(2, 2 * n // tiles) // 8) * 8
    slots = tiles * cap
    ext = cx + 2 * STEPS
    flat = control.reshape(chan, cx, ny)
    vmem = pl.BlockSpec(memory_space=pltpu.VMEM)
    smem = pl.BlockSpec(memory_space=pltpu.SMEM)
    hbm = pl.BlockSpec(memory_space=pl.ANY)
    face = jax.ShapeDtypeStruct((ext, 8, ny), F32)
    state = jax.ShapeDtypeStruct((chan, cx, ny), F32)
    dma = pltpu.SemaphoreType.DMA
    inc, back, cells, fxb, fyb, ocb = pl.pallas_call(
        functools.partial(observe_kernel, tiles, cap, chan, cx),
        out_shape=(
            state,
            jax.ShapeDtypeStruct((tiles, 3, cap, chan), F32),
            jax.ShapeDtypeStruct((3, 8, slots), I32),
            face, face, face,
        ),
        in_specs=[smem, hbm] + [vmem] * 6,
        out_specs=(hbm, hbm, vmem, vmem, vmem, vmem),
        scratch_shapes=[
            pltpu.VMEM((chan, cx, ny), F32),
            pltpu.VMEM((chan, STEPS, ny), F32),
            pltpu.VMEM((chan, STEPS, ny), F32),
            pltpu.VMEM((chan, cx, ny), F32),
            pltpu.VMEM((2, cx, ny), I32),
            pltpu.VMEM((2, STEPS, ny), I32),
            pltpu.VMEM((2, STEPS, ny), I32),
            pltpu.VMEM((3, 8, slots), I32),
            pltpu.VMEM((2, 8, slots), I32),
            pltpu.VMEM((cx // 2, 2 * ny, slots), BF16),
            pltpu.VMEM((chan, slots), F32),
            pltpu.VMEM((tiles, cap, MEMBERS * chan), F32),
            pltpu.VMEM((tiles, cap, MEMBERS * chan), F32),
            pltpu.VMEM((tiles, cap, chan), F32),
            pltpu.VMEM((tiles, cap, chan), F32),
            pltpu.VMEM((tiles + 2, cap, chan), F32),
            pltpu.VMEM((tiles, 3, cap, chan), F32),
            pltpu.VMEM((MEMBERS, slots, chan), F32),
            dma, dma((CHUNKS,)), dma, dma((2, CHUNKS)), dma((2, CHUNKS)), dma((4,)), dma((4,)), dma((3,)), dma((3,)),
        ],
        compiler_params=pltpu.CompilerParams(
            collective_id=0, has_side_effects=True, vmem_limit_bytes=48 * 2**20
        ),
        name="observe",
    )(class_table, flat, departures, obs_cell.reshape(1, n), obs_owner.reshape(1, n), scale_class, sea_mask, obs_precision)
    increment, gradient = pl.pallas_call(
        functools.partial(adjoint_kernel, chan, cx),
        out_shape=(state, state),
        in_specs=[hbm, hbm] + [vmem] * 5,
        out_specs=(hbm, hbm),
        scratch_shapes=[
            pltpu.VMEM((chan, cx, ny), F32),
            pltpu.VMEM((ext, chan, ny), F32),
            pltpu.VMEM((chan, cx, ny), F32),
            dma, dma, dma((CHUNKS,)),
        ],
        compiler_params=pltpu.CompilerParams(vmem_limit_bytes=48 * 2**20),
        name="adjoint",
    )(flat, inc, back, cells, fxb, fyb, ocb)
    return increment.reshape(control.shape), gradient.reshape(control.shape)


def solution(mesh):
    return jax.shard_map(
        body,
        mesh=mesh,
        in_specs=(
            P("groups", None, "tiles", None),
            P(("groups", "tiles"), None),
            P(("groups", "tiles")),
            P(("groups", "tiles"), None),
            P("tiles", None),
            P("tiles", None),
            P(),
            P("tiles", None),
        ),
        out_specs=(P("groups", None, "tiles", None), P("groups", None, "tiles", None)),
        check_vma=False,
    )
```

```python
import functools
import jax
import jax.numpy as jnp
from jax import lax
from jax.experimental import pallas as pl
from jax.experimental.pallas import tpu as pltpu
from jax.sharding import PartitionSpec as P

STEPS = 8
MEMBERS = 4
CHUNKS = 6
HIGHEST = lax.Precision.HIGHEST
F32 = jnp.float32
BF16 = jnp.bfloat16
I32 = jnp.int32


def split(x):
    high = x.astype(BF16)
    return high, (x - high.astype(F32)).astype(BF16)


def shifts(ny):
    row = lax.broadcasted_iota(I32, (ny, ny), 0)
    col = lax.broadcasted_iota(I32, (ny, ny), 1)
    both = jnp.concatenate(
        [jnp.where(row == col + 1, 1.0, 0.0).astype(BF16), jnp.where(row + 1 == col, 1.0, 0.0).astype(BF16)], axis=1
    )
    return jnp.concatenate([both, both], axis=0)


def sweep(state, faces, shift):
    count, ny = state[0].shape

    def face(which, r):
        return jnp.concatenate([faces[which, r]] * (count // 8), axis=0)

    for s in range(1, STEPS + 1):
        m = len(state)
        flux = [face(0, s - 1 + i) * (state[i + 1] - state[i]) for i in range(m - 1)]
        inner = jnp.concatenate(state[1:-1], axis=0)
        beside = jnp.dot(jnp.concatenate(split(inner), axis=1), shift, preferred_element_type=F32)
        after = []
        for i in range(1, m - 1):
            here = state[i]
            pair = beside[(i - 1) * count : i * count]
            change_y = face(1, s - 1 + i) * (pair[:, :ny] - here) + face(2, s - 1 + i) * (pair[:, ny:] - here)
            after.append(here + ((flux[i] - flux[i - 1]) + change_y))
        state = after
    return state


def observe_kernel(
    tiles, cap, chan, cx,
    table, control, departures, cell_ref, owner_ref, class_ref, mask_ref, precision_ref,
    inc_out, back_out, cells_out, faces, ocb,
    own, halo_l, halo_r, inc, geo, geo_l, geo_r, cells, cells_in, hot, model_t,
    dep_send, dep_recv, mod_send, mod_recv, ans, back, weighted_dep,
    local_sem, out_sem, back_sem, halo_send, halo_recv, geo_send, geo_recv, a2a_send, a2a_recv,
):
    me = lax.axis_index("tiles")
    h = STEPS
    ext = cx + 2 * h
    slots = tiles * cap
    nc = chan // CHUNKS
    ny = own.shape[2]
    right = lax.rem(me + 1, tiles)
    left = lax.rem(me + tiles - 1, tiles)

    own_copy = pltpu.make_async_copy(control, own, local_sem)
    own_copy.start()
    geo[0] = class_ref[...]
    geo[1] = mask_ref[...]

    barrier = pltpu.get_barrier_semaphore()

    @pl.loop(1, tiles)
    def _(k):
        pl.semaphore_signal(barrier, inc=1, device_id={"tiles": lax.rem(me + k, tiles)}, device_id_type=pl.DeviceIdType.MESH)

    pl.semaphore_wait(barrier, tiles - 1)

    def remote(src, dst, send, recv, to):
        return pltpu.make_async_remote_copy(
            src_ref=src, dst_ref=dst, send_sem=send, recv_sem=recv,
            device_id={"tiles": to}, device_id_type=pl.DeviceIdType.MESH,
        )

    geo_copies = [
        remote(geo.at[:, pl.ds(cx - h, h)], geo_l, geo_send.at[0], geo_recv.at[0], right),
        remote(geo.at[:, pl.ds(0, h)], geo_r, geo_send.at[1], geo_recv.at[1], left),
    ]
    for copy in geo_copies:
        copy.start()
    def halo_copy(side, q):
        part = pl.ds(q * nc, nc)
        if side == 0:
            return remote(control.at[part, pl.ds(cx - h, h)], halo_l.at[part], halo_send.at[0, q], halo_recv.at[0, q], right)
        return remote(control.at[part, pl.ds(0, h)], halo_r.at[part], halo_send.at[1, q], halo_recv.at[1, q], left)

    for q in range(CHUNKS):
        for side in range(2):
            halo_copy(side, q).start()

    n = departures.shape[0]
    eye = lax.broadcasted_iota(I32, (n, n), 0) == lax.broadcasted_iota(I32, (n, n), 1)
    lower = lax.broadcasted_iota(I32, (n, n), 1) < lax.broadcasted_iota(I32, (n, n), 0)
    owner_row = owner_ref[...]
    owner_col = jnp.sum(jnp.where(eye, owner_row, 0), axis=1, keepdims=True)
    cell_col = jnp.sum(jnp.where(eye, cell_ref[...], 0), axis=1, keepdims=True)
    slot_col = jnp.sum(jnp.where((owner_col == owner_row) & lower, 1, 0), axis=1, keepdims=True)
    offset = owner_col - me
    offset = jnp.where(offset < 0, offset + tiles, offset)
    dest_col = offset * cap + slot_col
    dest_row = jnp.sum(jnp.where(eye, dest_col, 0), axis=0, keepdims=True)
    place = jnp.where(lax.broadcasted_iota(I32, (slots, n), 0) == dest_row, 1.0, 0.0).astype(F32)
    spread = jnp.dot(place, departures[...], precision=HIGHEST, preferred_element_type=F32)
    dep_send[...] = spread.reshape(dep_send.shape)

    def exchange(src_of, dst, phase):
        @pl.loop(1, tiles)
        def _(k):
            src, to = src_of(k)
            remote(src, dst.at[k], a2a_send.at[phase], a2a_recv.at[phase], to).start()

    def landed(buffer, sem):
        pltpu.make_async_copy(buffer.at[pl.ds(1, tiles - 1)], buffer.at[pl.ds(1, tiles - 1)], sem).wait()

    exchange(lambda k: (dep_send.at[k], lax.rem(me + k, tiles)), dep_recv, 0)
    dep_recv[0] = dep_send[0]

    slot_lane = lax.broadcasted_iota(I32, (n, slots), 1)

    def cell_row(dest):
        return jnp.sum(jnp.where(dest == slot_lane, cell_col + 1, 0), axis=0, keepdims=True) - 1

    later = jnp.where(offset + 1 == tiles, 0, offset + 1) * cap + slot_col
    sooner = jnp.where(offset == 0, tiles - 1, offset - 1) * cap + slot_col
    mine = cell_row(dest_col)
    for j, row in enumerate((cell_row(later), mine, cell_row(sooner))):
        cells[j] = jnp.broadcast_to(row, cells.shape[1:])
    cell_copies = [
        remote(cells.at[0], cells_in.at[0], geo_send.at[2], geo_recv.at[2], left),
        remote(cells.at[2], cells_in.at[1], geo_send.at[3], geo_recv.at[3], right),
    ]
    for copy in cell_copies:
        copy.start()
    for j in range(cx // 2):
        index = lax.broadcasted_iota(I32, (2 * ny, slots), 0) + 2 * j * ny
        hot[j] = jnp.where(index == mine, 1.0, 0.0).astype(BF16)

    for copy in geo_copies:
        copy.wait()
    kinds = jnp.concatenate([geo_l[0], geo[0], geo_r[0]], axis=0)
    ocean = jnp.concatenate([geo_l[1], geo[1], geo_r[1]], axis=0).astype(F32)
    kx = jnp.zeros((ext, ny), F32)
    ky = jnp.zeros((ext, ny), F32)
    for c in range(table.shape[1]):
        kx = jnp.where(kinds == c, table[0, c], kx)
        ky = jnp.where(kinds == c, table[1, c], ky)
    face_x = 0.5 * (kx + pltpu.roll(kx, ext - 1, 0)) * ocean * pltpu.roll(ocean, ext - 1, 0)
    face_y = 0.5 * (ky + pltpu.roll(ky, ny - 1, 1)) * ocean * pltpu.roll(ocean, ny - 1, 1)
    face_y = jnp.where(lax.broadcasted_iota(I32, (ext, ny), 1) < ny - 1, face_y, 0.0)
    face_w = pltpu.roll(face_y, 1, 1)
    for r in range(ext):
        for which, array in enumerate((face_x, face_y, face_w)):
            faces[which, r] = jnp.broadcast_to(array[r : r + 1], (8, ny))
        ocb[r] = jnp.broadcast_to(ocean[r : r + 1], (8, ny))

    own_copy.wait()
    own2, left2, right2, inc2 = (
        own.reshape(chan * cx, ny), halo_l.reshape(chan * h, ny), halo_r.reshape(chan * h, ny), inc.reshape(chan * cx, ny)
    )
    shift = shifts(ny)

    @pl.loop(0, CHUNKS)
    def _(q):
        halo_copy(0, q).wait_recv()
        halo_copy(1, q).wait_recv()

        def load_row(i):
            if i < h:
                row = left2[pl.ds(q * nc * h + i, nc, stride=h), :]
            elif i < h + cx:
                row = own2[pl.ds(q * nc * cx + i - h, nc, stride=cx), :]
            else:
                row = right2[pl.ds(q * nc * h + i - h - cx, nc, stride=h), :]
            return jnp.concatenate([ocb[i]] * (nc // 8), axis=0) * row

        rows = sweep([load_row(i) for i in range(ext)], faces, shift)
        for r in range(cx):
            inc2[pl.ds(q * nc * cx + r, nc, stride=cx), :] = rows[r]
        part = pl.ds(q * nc, nc)
        pltpu.make_async_copy(inc.at[part], inc_out.at[part], out_sem.at[q]).start()
        total = jnp.zeros((nc, slots), F32)
        for j in range(cx // 2):
            for piece in split(jnp.concatenate(rows[2 * j : 2 * j + 2], axis=1)):
                total += jnp.dot(piece, hot[j], preferred_element_type=F32)
        model_t[part] = total

    mod_send[...] = model_t[...].T.reshape(mod_send.shape)
    exchange(lambda k: (mod_send.at[k], lax.rem(me + k, tiles)), mod_recv, 1)
    mod_recv[0] = mod_send[0]
    precision = precision_ref[...]
    landed(dep_recv, a2a_recv.at[0])
    for m in range(MEMBERS):
        rows = dep_recv[:, :, m * chan : (m + 1) * chan].reshape(slots, chan)
        weighted_dep[m] = jnp.dot(rows, precision, precision=HIGHEST, preferred_element_type=F32)
    landed(mod_recv, a2a_recv.at[1])
    model = mod_recv[...].reshape(slots, chan)
    weighted_model = jnp.dot(model, precision, precision=HIGHEST, preferred_element_type=F32)
    answer = jnp.zeros((slots, chan), F32)
    for m in range(MEMBERS):
        misfit = model - dep_recv[:, :, m * chan : (m + 1) * chan].reshape(slots, chan)
        weighted = weighted_model - weighted_dep[m]
        energy = jnp.sum(misfit * weighted, axis=1, keepdims=True) / chan
        answer += weighted / (1.0 + energy)
    answer = answer.reshape(tiles, cap, chan)
    ans[pl.ds(1, tiles)] = answer
    ans[0] = answer[tiles - 1]
    ans[tiles + 1] = answer[0]
    exchange(lambda k: (ans.at[pl.ds(k, 3)], lax.rem(me - k + tiles, tiles)), back, 2)
    for j in range(3):
        back[0, j] = ans[j]
    for copy in cell_copies:
        copy.wait()
    cells_out[0] = cells_in[0]
    cells_out[1] = cells[1]
    cells_out[2] = cells_in[1]
    for q in range(CHUNKS):
        for side in range(2):
            halo_copy(side, q).wait_send()
    landed(dep_recv, a2a_send.at[0])
    landed(mod_recv, a2a_send.at[1])
    for q in range(CHUNKS):
        part = pl.ds(q * nc, nc)
        pltpu.make_async_copy(inc.at[part], inc_out.at[part], out_sem.at[q]).wait()
    landed(back, a2a_recv.at[2])
    landed(back, a2a_send.at[2])
    copy = pltpu.make_async_copy(back, back_out, back_sem)
    copy.start()
    copy.wait()


def adjoint_kernel(
    chan, cx,
    control, inc_in, back, cells, faces, ocb,
    inc_out, grad_out,
    own, field, grad, inc_sem, own_sem, out_sem,
):
    h = STEPS
    ext = cx + 2 * h
    ny = own.shape[2]
    nc = chan // CHUNKS
    tiles, _, cap, _ = back.shape
    slots = tiles * cap
    own_copy = pltpu.make_async_copy(control, own, own_sem)
    own_copy.start()
    inc_copy = pltpu.make_async_copy(inc_in, inc_out, inc_sem)
    inc_copy.start()
    eye = lax.broadcasted_iota(I32, (slots, slots), 0) == lax.broadcasted_iota(I32, (slots, slots), 1)
    for j, start, first, count in ((1, h, 0, cx), (0, h + cx, 0, h), (2, 0, cx - h, h)):
        rows_t = back[:, j].reshape(slots, chan).T
        lhs = jnp.concatenate(split(rows_t), axis=1)
        cell = jnp.sum(jnp.where(eye, cells[j, 0:1], 0), axis=1, keepdims=True)
        for x in range(0, count, 2):
            index = lax.broadcasted_iota(I32, (slots, 2 * ny), 1) + (first + x) * ny
            hot = jnp.where(index == cell, 1.0, 0.0).astype(BF16)
            out = jnp.dot(lhs, jnp.concatenate([hot, hot], axis=0), preferred_element_type=F32)
            field[start + x] = out[:, :ny]
            field[start + x + 1] = out[:, ny:]
    own_copy.wait()
    own2, grad2 = own.reshape(chan * cx, ny), grad.reshape(chan * cx, ny)
    shift = shifts(ny)

    def out_copy(q):
        part = pl.ds(q * nc, nc)
        return pltpu.make_async_copy(grad.at[part], grad_out.at[part], out_sem.at[q])

    @pl.loop(0, CHUNKS)
    def _(q):
        rows = sweep([field[i, pl.ds(pl.multiple_of(q * nc, nc), nc), :] for i in range(ext)], faces, shift)
        for r in range(cx):
            at = pl.ds(q * nc * cx + r, nc, stride=cx)
            grad2[at, :] = own2[at, :] + jnp.concatenate([ocb[r + h]] * (nc // 8), axis=0) * rows[r]
        out_copy(q).start()

    for q in range(CHUNKS):
        out_copy(q).wait()
    inc_copy.wait()


def body(control, departures, obs_cell, obs_owner, scale_class, sea_mask, class_table, obs_precision):
    fields, levels, cx, ny = control.shape
    chan = fields * levels
    n = obs_cell.shape[0]
    tiles = lax.axis_size("tiles")
    cap = -(-max(2, 2 * n // tiles) // 8) * 8
    slots = tiles * cap
    ext = cx + 2 * STEPS
    flat = control.reshape(chan, cx, ny)
    vmem = pl.BlockSpec(memory_space=pltpu.VMEM)
    smem = pl.BlockSpec(memory_space=pltpu.SMEM)
    hbm = pl.BlockSpec(memory_space=pl.ANY)
    state = jax.ShapeDtypeStruct((chan, cx, ny), F32)
    dma = pltpu.SemaphoreType.DMA
    inc, back, cells, faces, ocb = pl.pallas_call(
        functools.partial(observe_kernel, tiles, cap, chan, cx),
        out_shape=(
            state,
            jax.ShapeDtypeStruct((tiles, 3, cap, chan), F32),
            jax.ShapeDtypeStruct((3, 8, slots), I32),
            jax.ShapeDtypeStruct((3, ext, 8, ny), F32),
            jax.ShapeDtypeStruct((ext, 8, ny), F32),
        ),
        in_specs=[smem, hbm] + [vmem] * 6,
        out_specs=(hbm, hbm, vmem, vmem, vmem),
        scratch_shapes=[
            pltpu.VMEM((chan, cx, ny), F32),
            pltpu.VMEM((chan, STEPS, ny), F32),
            pltpu.VMEM((chan, STEPS, ny), F32),
            pltpu.VMEM((chan, cx, ny), F32),
            pltpu.VMEM((2, cx, ny), I32),
            pltpu.VMEM((2, STEPS, ny), I32),
            pltpu.VMEM((2, STEPS, ny), I32),
            pltpu.VMEM((3, 8, slots), I32),
            pltpu.VMEM((2, 8, slots), I32),
            pltpu.VMEM((cx // 2, 2 * ny, slots), BF16),
            pltpu.VMEM((chan, slots), F32),
            pltpu.VMEM((tiles, cap, MEMBERS * chan), F32),
            pltpu.VMEM((tiles, cap, MEMBERS * chan), F32),
            pltpu.VMEM((tiles, cap, chan), F32),
            pltpu.VMEM((tiles, cap, chan), F32),
            pltpu.VMEM((tiles + 2, cap, chan), F32),
            pltpu.VMEM((tiles, 3, cap, chan), F32),
            pltpu.VMEM((MEMBERS, slots, chan), F32),
            dma, dma((CHUNKS,)), dma, dma((2, CHUNKS)), dma((2, CHUNKS)), dma((4,)), dma((4,)), dma((3,)), dma((3,)),
        ],
        compiler_params=pltpu.CompilerParams(
            collective_id=0, has_side_effects=True, vmem_limit_bytes=63 * 2**20
        ),
        name="observe",
    )(class_table, flat, departures, obs_cell.reshape(1, n), obs_owner.reshape(1, n), scale_class, sea_mask, obs_precision)
    increment, gradient = pl.pallas_call(
        functools.partial(adjoint_kernel, chan, cx),
        out_shape=(state, state),
        in_specs=[hbm, hbm] + [vmem] * 4,
        out_specs=(hbm, hbm),
        scratch_shapes=[
            pltpu.VMEM((chan, cx, ny), F32),
            pltpu.VMEM((ext, chan, ny), F32),
            pltpu.VMEM((chan, cx, ny), F32),
            dma, dma, dma((CHUNKS,)),
        ],
        compiler_params=pltpu.CompilerParams(vmem_limit_bytes=63 * 2**20),
        name="adjoint",
    )(flat, inc, back, cells, faces, ocb)
    return increment.reshape(control.shape), gradient.reshape(control.shape)


def solution(mesh):
    return jax.shard_map(
        body,
        mesh=mesh,
        in_specs=(
            P("groups", None, "tiles", None),
            P(("groups", "tiles"), None),
            P(("groups", "tiles")),
            P(("groups", "tiles"), None),
            P("tiles", None),
            P("tiles", None),
            P(),
            P("tiles", None),
        ),
        out_specs=(P("groups", None, "tiles", None), P("groups", None, "tiles", None)),
        check_vma=False,
    )
```

```python
import functools
import jax
import jax.numpy as jnp
from jax import lax
from jax.experimental import pallas as pl
from jax.experimental.pallas import tpu as pltpu
from jax.sharding import PartitionSpec as P

STEPS = 8
MEMBERS = 4
CHUNKS = 6
HIGHEST = lax.Precision.HIGHEST
F32 = jnp.float32
BF16 = jnp.bfloat16
I32 = jnp.int32


def split(x):
    high = x.astype(BF16)
    return high, (x - high.astype(F32)).astype(BF16)


def shifts(ny):
    row = lax.broadcasted_iota(I32, (ny, ny), 0)
    col = lax.broadcasted_iota(I32, (ny, ny), 1)
    both = jnp.concatenate(
        [jnp.where(row == col + 1, 1.0, 0.0).astype(BF16), jnp.where(row + 1 == col, 1.0, 0.0).astype(BF16)], axis=1
    )
    return jnp.concatenate([both, both], axis=0)


def sweep(state, faces, shift):
    count, ny = state[0].shape

    def face(which, r):
        return jnp.concatenate([faces[which, r]] * (count // 8), axis=0)

    for s in range(1, STEPS + 1):
        m = len(state)
        flux = [face(0, s - 1 + i) * (state[i + 1] - state[i]) for i in range(m - 1)]
        inner = jnp.concatenate(state[1:-1], axis=0)
        beside = jnp.dot(jnp.concatenate(split(inner), axis=1), shift, preferred_element_type=F32)
        after = []
        for i in range(1, m - 1):
            here = state[i]
            pair = beside[(i - 1) * count : i * count]
            change_y = face(1, s - 1 + i) * (pair[:, :ny] - here) + face(2, s - 1 + i) * (pair[:, ny:] - here)
            after.append(here + ((flux[i] - flux[i - 1]) + change_y))
        state = after
    return state


def observe_kernel(
    tiles, cap, chan, cx,
    table, control, departures, cell_ref, owner_ref, class_ref, mask_ref, precision_ref,
    inc_out, back_out, cells_out, faces, ocb,
    own, halo_l, halo_r, inc, geo, geo_l, geo_r, cells, cells_in, hot, model_t,
    dep_send, dep_recv, mod_send, mod_recv, ans, back, weighted_dep,
    local_sem, out_sem, back_sem, halo_send, halo_recv, geo_send, geo_recv, a2a_send, a2a_recv,
):
    me = lax.axis_index("tiles")
    h = STEPS
    ext = cx + 2 * h
    slots = tiles * cap
    nc = chan // CHUNKS
    ny = own.shape[2]
    right = lax.rem(me + 1, tiles)
    left = lax.rem(me + tiles - 1, tiles)

    own_copy = pltpu.make_async_copy(control, own, local_sem)
    own_copy.start()
    geo[0] = class_ref[...]
    geo[1] = mask_ref[...]

    barrier = pltpu.get_barrier_semaphore()

    @pl.loop(1, tiles)
    def _(k):
        pl.semaphore_signal(barrier, inc=1, device_id={"tiles": lax.rem(me + k, tiles)}, device_id_type=pl.DeviceIdType.MESH)

    pl.semaphore_wait(barrier, tiles - 1)

    def remote(src, dst, send, recv, to):
        return pltpu.make_async_remote_copy(
            src_ref=src, dst_ref=dst, send_sem=send, recv_sem=recv,
            device_id={"tiles": to}, device_id_type=pl.DeviceIdType.MESH,
        )

    geo_copies = [
        remote(geo.at[:, pl.ds(cx - h, h)], geo_l, geo_send.at[0], geo_recv.at[0], right),
        remote(geo.at[:, pl.ds(0, h)], geo_r, geo_send.at[1], geo_recv.at[1], left),
    ]
    for copy in geo_copies:
        copy.start()
    def halo_copy(side, q):
        part = pl.ds(q * nc, nc)
        if side == 0:
            return remote(control.at[part, pl.ds(cx - h, h)], halo_l.at[part], halo_send.at[0, q], halo_recv.at[0, q], right)
        return remote(control.at[part, pl.ds(0, h)], halo_r.at[part], halo_send.at[1, q], halo_recv.at[1, q], left)

    for q in range(CHUNKS):
        for side in range(2):
            halo_copy(side, q).start()

    n = departures.shape[0]
    eye = lax.broadcasted_iota(I32, (n, n), 0) == lax.broadcasted_iota(I32, (n, n), 1)
    lower = lax.broadcasted_iota(I32, (n, n), 1) < lax.broadcasted_iota(I32, (n, n), 0)
    owner_row = owner_ref[...]
    owner_col = jnp.sum(jnp.where(eye, owner_row, 0), axis=1, keepdims=True)
    cell_col = jnp.sum(jnp.where(eye, cell_ref[...], 0), axis=1, keepdims=True)
    slot_col = jnp.sum(jnp.where((owner_col == owner_row) & lower, 1, 0), axis=1, keepdims=True)
    offset = owner_col - me
    offset = jnp.where(offset < 0, offset + tiles, offset)
    dest_col = offset * cap + slot_col
    dest_row = jnp.sum(jnp.where(eye, dest_col, 0), axis=0, keepdims=True)
    place = jnp.where(lax.broadcasted_iota(I32, (slots, n), 0) == dest_row, 1.0, 0.0).astype(F32)
    spread = jnp.dot(place, departures[...], precision=HIGHEST, preferred_element_type=F32)
    dep_send[...] = spread.reshape(dep_send.shape)

    def exchange(src_of, dst, phase):
        @pl.loop(1, tiles)
        def _(k):
            src, to = src_of(k)
            remote(src, dst.at[k], a2a_send.at[phase], a2a_recv.at[phase], to).start()

    def landed(buffer, sem):
        pltpu.make_async_copy(buffer.at[pl.ds(1, tiles - 1)], buffer.at[pl.ds(1, tiles - 1)], sem).wait()

    exchange(lambda k: (dep_send.at[k], lax.rem(me + k, tiles)), dep_recv, 0)
    dep_recv[0] = dep_send[0]

    slot_lane = lax.broadcasted_iota(I32, (n, slots), 1)

    def cell_row(dest):
        return jnp.sum(jnp.where(dest == slot_lane, cell_col + 1, 0), axis=0, keepdims=True) - 1

    later = jnp.where(offset + 1 == tiles, 0, offset + 1) * cap + slot_col
    sooner = jnp.where(offset == 0, tiles - 1, offset - 1) * cap + slot_col
    mine = cell_row(dest_col)
    for j, row in enumerate((cell_row(later), mine, cell_row(sooner))):
        cells[j] = jnp.broadcast_to(row, cells.shape[1:])
    cell_copies = [
        remote(cells.at[0], cells_in.at[0], geo_send.at[2], geo_recv.at[2], left),
        remote(cells.at[2], cells_in.at[1], geo_send.at[3], geo_recv.at[3], right),
    ]
    for copy in cell_copies:
        copy.start()
    for j in range(cx // 2):
        index = lax.broadcasted_iota(I32, (2 * ny, slots), 0) + 2 * j * ny
        hot[j] = jnp.where(index == mine, 1.0, 0.0).astype(BF16)

    for copy in geo_copies:
        copy.wait()
    kinds = jnp.concatenate([geo_l[0], geo[0], geo_r[0]], axis=0)
    ocean = jnp.concatenate([geo_l[1], geo[1], geo_r[1]], axis=0).astype(F32)
    kx = jnp.zeros((ext, ny), F32)
    ky = jnp.zeros((ext, ny), F32)
    for c in range(table.shape[1]):
        kx = jnp.where(kinds == c, table[0, c], kx)
        ky = jnp.where(kinds == c, table[1, c], ky)
    face_x = 0.5 * (kx + pltpu.roll(kx, ext - 1, 0)) * ocean * pltpu.roll(ocean, ext - 1, 0)
    face_y = 0.5 * (ky + pltpu.roll(ky, ny - 1, 1)) * ocean * pltpu.roll(ocean, ny - 1, 1)
    face_y = jnp.where(lax.broadcasted_iota(I32, (ext, ny), 1) < ny - 1, face_y, 0.0)
    face_w = pltpu.roll(face_y, 1, 1)
    for r in range(ext):
        for which, array in enumerate((face_x, face_y, face_w)):
            faces[which, r] = jnp.broadcast_to(array[r : r + 1], (8, ny))
        ocb[r] = jnp.broadcast_to(ocean[r : r + 1], (8, ny))

    own_copy.wait()
    own2, left2, right2, inc2 = (
        own.reshape(chan * cx, ny), halo_l.reshape(chan * h, ny), halo_r.reshape(chan * h, ny), inc.reshape(chan * cx, ny)
    )
    shift = shifts(ny)

    @pl.loop(0, CHUNKS)
    def _(q):
        halo_copy(0, q).wait_recv()
        halo_copy(1, q).wait_recv()

        def load_row(i):
            if i < h:
                row = left2[pl.ds(q * nc * h + i, nc, stride=h), :]
            elif i < h + cx:
                row = own2[pl.ds(q * nc * cx + i - h, nc, stride=cx), :]
            else:
                row = right2[pl.ds(q * nc * h + i - h - cx, nc, stride=h), :]
            return jnp.concatenate([ocb[i]] * (nc // 8), axis=0) * row

        rows = sweep([load_row(i) for i in range(ext)], faces, shift)
        for r in range(cx):
            inc2[pl.ds(q * nc * cx + r, nc, stride=cx), :] = rows[r]
        part = pl.ds(q * nc, nc)
        pltpu.make_async_copy(inc.at[part], inc_out.at[part], out_sem.at[q]).start()
        total = jnp.zeros((nc, slots), F32)
        for j in range(cx // 2):
            for piece in split(jnp.concatenate(rows[2 * j : 2 * j + 2], axis=1)):
                total += jnp.dot(piece, hot[j], preferred_element_type=F32)
        model_t[part] = total

    mod_send[...] = model_t[...].T.reshape(mod_send.shape)
    exchange(lambda k: (mod_send.at[k], lax.rem(me + k, tiles)), mod_recv, 1)
    mod_recv[0] = mod_send[0]
    precision = precision_ref[...]
    landed(dep_recv, a2a_recv.at[0])
    for m in range(MEMBERS):
        rows = dep_recv[:, :, m * chan : (m + 1) * chan].reshape(slots, chan)
        weighted_dep[m] = jnp.dot(rows, precision, precision=HIGHEST, preferred_element_type=F32)
    landed(mod_recv, a2a_recv.at[1])
    model = mod_recv[...].reshape(slots, chan)
    weighted_model = jnp.dot(model, precision, precision=HIGHEST, preferred_element_type=F32)
    answer = jnp.zeros((slots, chan), F32)
    for m in range(MEMBERS):
        misfit = model - dep_recv[:, :, m * chan : (m + 1) * chan].reshape(slots, chan)
        weighted = weighted_model - weighted_dep[m]
        energy = jnp.sum(misfit * weighted, axis=1, keepdims=True) / chan
        answer += weighted / (1.0 + energy)
    answer = answer.reshape(tiles, cap, chan)
    ans[pl.ds(1, tiles)] = answer
    ans[0] = answer[tiles - 1]
    ans[tiles + 1] = answer[0]
    exchange(lambda k: (ans.at[pl.ds(k, 3)], lax.rem(me - k + tiles, tiles)), back, 2)
    for j in range(3):
        back[0, j] = ans[j]
    for copy in cell_copies:
        copy.wait()
    cells_out[0] = cells_in[0]
    cells_out[1] = cells[1]
    cells_out[2] = cells_in[1]
    for q in range(CHUNKS):
        for side in range(2):
            halo_copy(side, q).wait_send()
    landed(dep_recv, a2a_send.at[0])
    landed(mod_recv, a2a_send.at[1])
    for q in range(CHUNKS):
        part = pl.ds(q * nc, nc)
        pltpu.make_async_copy(inc.at[part], inc_out.at[part], out_sem.at[q]).wait()
    landed(back, a2a_recv.at[2])
    landed(back, a2a_send.at[2])
    copy = pltpu.make_async_copy(back, back_out, back_sem)
    copy.start()
    copy.wait()


def adjoint_kernel(
    chan, cx,
    control, inc_in, back, cells, faces, ocb,
    inc_out, grad_out,
    own, field, grad, inc, inc_sem, own_sem, out_sem,
):
    h = STEPS
    ext = cx + 2 * h
    ny = own.shape[2]
    nc = chan // CHUNKS
    tiles, _, cap, _ = back.shape
    slots = tiles * cap
    own_copy = pltpu.make_async_copy(control, own, own_sem)
    own_copy.start()
    inc_copy = pltpu.make_async_copy(inc_in, inc, inc_sem)
    inc_copy.start()
    eye = lax.broadcasted_iota(I32, (slots, slots), 0) == lax.broadcasted_iota(I32, (slots, slots), 1)
    for j, start, first, count in ((1, h, 0, cx), (0, h + cx, 0, h), (2, 0, cx - h, h)):
        rows_t = back[:, j].reshape(slots, chan).T
        lhs = jnp.concatenate(split(rows_t), axis=1)
        cell = jnp.sum(jnp.where(eye, cells[j, 0:1], 0), axis=1, keepdims=True)
        for x in range(0, count, 2):
            index = lax.broadcasted_iota(I32, (slots, 2 * ny), 1) + (first + x) * ny
            hot = jnp.where(index == cell, 1.0, 0.0).astype(BF16)
            out = jnp.dot(lhs, jnp.concatenate([hot, hot], axis=0), preferred_element_type=F32)
            field[start + x] = out[:, :ny]
            field[start + x + 1] = out[:, ny:]
    own_copy.wait()
    inc_copy.wait()
    inc_copy = pltpu.make_async_copy(inc, inc_out, inc_sem)
    inc_copy.start()
    own2, grad2 = own.reshape(chan * cx, ny), grad.reshape(chan * cx, ny)
    shift = shifts(ny)

    def out_copy(q):
        part = pl.ds(q * nc, nc)
        return pltpu.make_async_copy(grad.at[part], grad_out.at[part], out_sem.at[q])

    @pl.loop(0, CHUNKS)
    def _(q):
        rows = sweep([field[i, pl.ds(pl.multiple_of(q * nc, nc), nc), :] for i in range(ext)], faces, shift)
        for r in range(cx):
            at = pl.ds(q * nc * cx + r, nc, stride=cx)
            grad2[at, :] = own2[at, :] + jnp.concatenate([ocb[r + h]] * (nc // 8), axis=0) * rows[r]
        out_copy(q).start()

    for q in range(CHUNKS):
        out_copy(q).wait()
    inc_copy.wait()


def body(control, departures, obs_cell, obs_owner, scale_class, sea_mask, class_table, obs_precision):
    fields, levels, cx, ny = control.shape
    chan = fields * levels
    n = obs_cell.shape[0]
    tiles = lax.axis_size("tiles")
    cap = -(-max(2, 2 * n // tiles) // 8) * 8
    slots = tiles * cap
    ext = cx + 2 * STEPS
    flat = control.reshape(chan, cx, ny)
    vmem = pl.BlockSpec(memory_space=pltpu.VMEM)
    smem = pl.BlockSpec(memory_space=pltpu.SMEM)
    hbm = pl.BlockSpec(memory_space=pl.ANY)
    state = jax.ShapeDtypeStruct((chan, cx, ny), F32)
    dma = pltpu.SemaphoreType.DMA
    inc, back, cells, faces, ocb = pl.pallas_call(
        functools.partial(observe_kernel, tiles, cap, chan, cx),
        out_shape=(
            state,
            jax.ShapeDtypeStruct((tiles, 3, cap, chan), F32),
            jax.ShapeDtypeStruct((3, 8, slots), I32),
            jax.ShapeDtypeStruct((3, ext, 8, ny), F32),
            jax.ShapeDtypeStruct((ext, 8, ny), F32),
        ),
        in_specs=[smem, hbm] + [vmem] * 6,
        out_specs=(hbm, hbm, vmem, vmem, vmem),
        scratch_shapes=[
            pltpu.VMEM((chan, cx, ny), F32),
            pltpu.VMEM((chan, STEPS, ny), F32),
            pltpu.VMEM((chan, STEPS, ny), F32),
            pltpu.VMEM((chan, cx, ny), F32),
            pltpu.VMEM((2, cx, ny), I32),
            pltpu.VMEM((2, STEPS, ny), I32),
            pltpu.VMEM((2, STEPS, ny), I32),
            pltpu.VMEM((3, 8, slots), I32),
            pltpu.VMEM((2, 8, slots), I32),
            pltpu.VMEM((cx // 2, 2 * ny, slots), BF16),
            pltpu.VMEM((chan, slots), F32),
            pltpu.VMEM((tiles, cap, MEMBERS * chan), F32),
            pltpu.VMEM((tiles, cap, MEMBERS * chan), F32),
            pltpu.VMEM((tiles, cap, chan), F32),
            pltpu.VMEM((tiles, cap, chan), F32),
            pltpu.VMEM((tiles + 2, cap, chan), F32),
            pltpu.VMEM((tiles, 3, cap, chan), F32),
            pltpu.VMEM((MEMBERS, slots, chan), F32),
            dma, dma((CHUNKS,)), dma, dma((2, CHUNKS)), dma((2, CHUNKS)), dma((4,)), dma((4,)), dma((3,)), dma((3,)),
        ],
        compiler_params=pltpu.CompilerParams(
            collective_id=0, has_side_effects=True, vmem_limit_bytes=63 * 2**20
        ),
        name="observe",
    )(class_table, flat, departures, obs_cell.reshape(1, n), obs_owner.reshape(1, n), scale_class, sea_mask, obs_precision)
    increment, gradient = pl.pallas_call(
        functools.partial(adjoint_kernel, chan, cx),
        out_shape=(state, state),
        in_specs=[hbm, hbm] + [vmem] * 4,
        out_specs=(hbm, hbm),
        scratch_shapes=[
            pltpu.VMEM((chan, cx, ny), F32),
            pltpu.VMEM((ext, chan, ny), F32),
            pltpu.VMEM((chan, cx, ny), F32),
            pltpu.VMEM((chan, cx, ny), F32),
            dma, dma, dma((CHUNKS,)),
        ],
        compiler_params=pltpu.CompilerParams(vmem_limit_bytes=63 * 2**20),
        name="adjoint",
    )(flat, inc, back, cells, faces, ocb)
    return increment.reshape(control.shape), gradient.reshape(control.shape)


def solution(mesh):
    return jax.shard_map(
        body,
        mesh=mesh,
        in_specs=(
            P("groups", None, "tiles", None),
            P(("groups", "tiles"), None),
            P(("groups", "tiles")),
            P(("groups", "tiles"), None),
            P("tiles", None),
            P("tiles", None),
            P(),
            P("tiles", None),
        ),
        out_specs=(P("groups", None, "tiles", None), P("groups", None, "tiles", None)),
        check_vma=False,
    )
```

```python
import functools
import jax
import jax.numpy as jnp
from jax import lax
from jax.experimental import pallas as pl
from jax.experimental.pallas import tpu as pltpu
from jax.sharding import PartitionSpec as P

STEPS = 8
MEMBERS = 4
CHUNKS = 6
HIGHEST = lax.Precision.HIGHEST
F32 = jnp.float32
BF16 = jnp.bfloat16
I32 = jnp.int32


def split(x):
    high = x.astype(BF16)
    return high, (x - high.astype(F32)).astype(BF16)


def shifts(ny):
    row = lax.broadcasted_iota(I32, (ny, ny), 0)
    col = lax.broadcasted_iota(I32, (ny, ny), 1)
    both = jnp.concatenate(
        [jnp.where(row == col + 1, 1.0, 0.0).astype(BF16), jnp.where(row + 1 == col, 1.0, 0.0).astype(BF16)], axis=1
    )
    return jnp.concatenate([both, both], axis=0)


def sweep(state, faces, shift):
    count, ny = state[0].shape

    def face(which, r):
        return jnp.concatenate([faces[which, r]] * (count // 8), axis=0)

    for s in range(1, STEPS + 1):
        m = len(state)
        flux = [face(0, s - 1 + i) * (state[i + 1] - state[i]) for i in range(m - 1)]
        inner = jnp.concatenate(state[1:-1], axis=0)
        beside = jnp.dot(jnp.concatenate(split(inner), axis=1), shift, preferred_element_type=F32)
        after = []
        for i in range(1, m - 1):
            here = state[i]
            pair = beside[(i - 1) * count : i * count]
            change_y = face(1, s - 1 + i) * (pair[:, :ny] - here) + face(2, s - 1 + i) * (pair[:, ny:] - here)
            after.append(here + ((flux[i] - flux[i - 1]) + change_y))
        state = after
    return state


def observe_kernel(
    tiles, cap, chan, cx,
    table, control, departures, cell_ref, owner_ref, class_ref, mask_ref, precision_ref,
    inc_out, back_out, cells_out, faces, ocb,
    own, halo_l, halo_r, inc, geo, geo_l, geo_r, cells, cells_in, hot, model_t,
    dep_send, dep_recv, mod_send, mod_recv, ans, back, back_l, back_r, weighted_dep,
    local_sem, out_sem, back_sem, halo_send, halo_recv, geo_send, geo_recv, a2a_send, a2a_recv,
):
    me = lax.axis_index("tiles")
    h = STEPS
    ext = cx + 2 * h
    slots = tiles * cap
    nc = chan // CHUNKS
    ny = own.shape[2]
    right = lax.rem(me + 1, tiles)
    left = lax.rem(me + tiles - 1, tiles)

    own_copy = pltpu.make_async_copy(control, own, local_sem)
    own_copy.start()
    geo[0] = class_ref[...]
    geo[1] = mask_ref[...]

    barrier = pltpu.get_barrier_semaphore()

    @pl.loop(1, tiles)
    def _(k):
        pl.semaphore_signal(barrier, inc=1, device_id={"tiles": lax.rem(me + k, tiles)}, device_id_type=pl.DeviceIdType.MESH)

    pl.semaphore_wait(barrier, tiles - 1)

    def remote(src, dst, send, recv, to):
        return pltpu.make_async_remote_copy(
            src_ref=src, dst_ref=dst, send_sem=send, recv_sem=recv,
            device_id={"tiles": to}, device_id_type=pl.DeviceIdType.MESH,
        )

    geo_copies = [
        remote(geo.at[:, pl.ds(cx - h, h)], geo_l, geo_send.at[0], geo_recv.at[0], right),
        remote(geo.at[:, pl.ds(0, h)], geo_r, geo_send.at[1], geo_recv.at[1], left),
    ]
    for copy in geo_copies:
        copy.start()
    def halo_copy(side, q):
        part = pl.ds(q * nc, nc)
        if side == 0:
            return remote(control.at[part, pl.ds(cx - h, h)], halo_l.at[part], halo_send.at[0, q], halo_recv.at[0, q], right)
        return remote(control.at[part, pl.ds(0, h)], halo_r.at[part], halo_send.at[1, q], halo_recv.at[1, q], left)

    for q in range(CHUNKS):
        for side in range(2):
            halo_copy(side, q).start()

    n = departures.shape[0]
    eye = lax.broadcasted_iota(I32, (n, n), 0) == lax.broadcasted_iota(I32, (n, n), 1)
    lower = lax.broadcasted_iota(I32, (n, n), 1) < lax.broadcasted_iota(I32, (n, n), 0)
    owner_row = owner_ref[...]
    owner_col = jnp.sum(jnp.where(eye, owner_row, 0), axis=1, keepdims=True)
    cell_col = jnp.sum(jnp.where(eye, cell_ref[...], 0), axis=1, keepdims=True)
    slot_col = jnp.sum(jnp.where((owner_col == owner_row) & lower, 1, 0), axis=1, keepdims=True)
    offset = owner_col - me
    offset = jnp.where(offset < 0, offset + tiles, offset)
    dest_col = offset * cap + slot_col
    dest_row = jnp.sum(jnp.where(eye, dest_col, 0), axis=0, keepdims=True)
    place = jnp.where(lax.broadcasted_iota(I32, (slots, n), 0) == dest_row, 1.0, 0.0).astype(F32)
    spread = jnp.dot(place, departures[...], precision=HIGHEST, preferred_element_type=F32)
    dep_send[...] = spread.reshape(dep_send.shape)

    def exchange(src_of, dst, phase):
        @pl.loop(1, tiles)
        def _(k):
            src, to = src_of(k)
            remote(src, dst.at[k], a2a_send.at[phase], a2a_recv.at[phase], to).start()

    def landed(buffer, sem):
        pltpu.make_async_copy(buffer.at[pl.ds(1, tiles - 1)], buffer.at[pl.ds(1, tiles - 1)], sem).wait()

    exchange(lambda k: (dep_send.at[k], lax.rem(me + k, tiles)), dep_recv, 0)
    dep_recv[0] = dep_send[0]

    slot_lane = lax.broadcasted_iota(I32, (n, slots), 1)

    def cell_row(dest):
        return jnp.sum(jnp.where(dest == slot_lane, cell_col + 1, 0), axis=0, keepdims=True) - 1

    mine = cell_row(dest_col)
    for j in range(3):
        cells[j] = jnp.broadcast_to(mine, cells.shape[1:])
    cell_copies = [
        remote(cells.at[0], cells_in.at[0], geo_send.at[2], geo_recv.at[2], left),
        remote(cells.at[2], cells_in.at[1], geo_send.at[3], geo_recv.at[3], right),
    ]
    for copy in cell_copies:
        copy.start()
    for j in range(cx // 2):
        index = lax.broadcasted_iota(I32, (2 * ny, slots), 0) + 2 * j * ny
        hot[j] = jnp.where(index == mine, 1.0, 0.0).astype(BF16)

    for copy in geo_copies:
        copy.wait()
    kinds = jnp.concatenate([geo_l[0], geo[0], geo_r[0]], axis=0)
    ocean = jnp.concatenate([geo_l[1], geo[1], geo_r[1]], axis=0).astype(F32)
    kx = jnp.zeros((ext, ny), F32)
    ky = jnp.zeros((ext, ny), F32)
    for c in range(table.shape[1]):
        kx = jnp.where(kinds == c, table[0, c], kx)
        ky = jnp.where(kinds == c, table[1, c], ky)
    face_x = 0.5 * (kx + pltpu.roll(kx, ext - 1, 0)) * ocean * pltpu.roll(ocean, ext - 1, 0)
    face_y = 0.5 * (ky + pltpu.roll(ky, ny - 1, 1)) * ocean * pltpu.roll(ocean, ny - 1, 1)
    face_y = jnp.where(lax.broadcasted_iota(I32, (ext, ny), 1) < ny - 1, face_y, 0.0)
    face_w = pltpu.roll(face_y, 1, 1)
    for r in range(ext):
        for which, array in enumerate((face_x, face_y, face_w)):
            faces[which, r] = jnp.broadcast_to(array[r : r + 1], (8, ny))
        ocb[r] = jnp.broadcast_to(ocean[r : r + 1], (8, ny))

    own_copy.wait()
    own2, left2, right2, inc2 = (
        own.reshape(chan * cx, ny), halo_l.reshape(chan * h, ny), halo_r.reshape(chan * h, ny), inc.reshape(chan * cx, ny)
    )
    shift = shifts(ny)

    @pl.loop(0, CHUNKS)
    def _(q):
        halo_copy(0, q).wait_recv()
        halo_copy(1, q).wait_recv()

        def load_row(i):
            if i < h:
                row = left2[pl.ds(q * nc * h + i, nc, stride=h), :]
            elif i < h + cx:
                row = own2[pl.ds(q * nc * cx + i - h, nc, stride=cx), :]
            else:
                row = right2[pl.ds(q * nc * h + i - h - cx, nc, stride=h), :]
            return jnp.concatenate([ocb[i]] * (nc // 8), axis=0) * row

        rows = sweep([load_row(i) for i in range(ext)], faces, shift)
        for r in range(cx):
            inc2[pl.ds(q * nc * cx + r, nc, stride=cx), :] = rows[r]
        part = pl.ds(q * nc, nc)
        pltpu.make_async_copy(inc.at[part], inc_out.at[part], out_sem.at[q]).start()
        total = jnp.zeros((nc, slots), F32)
        for j in range(cx // 2):
            for piece in split(jnp.concatenate(rows[2 * j : 2 * j + 2], axis=1)):
                total += jnp.dot(piece, hot[j], preferred_element_type=F32)
        model_t[part] = total

    mod_send[...] = model_t[...].T.reshape(mod_send.shape)
    exchange(lambda k: (mod_send.at[k], lax.rem(me + k, tiles)), mod_recv, 1)
    mod_recv[0] = mod_send[0]
    precision = precision_ref[...]
    landed(dep_recv, a2a_recv.at[0])
    for m in range(MEMBERS):
        rows = dep_recv[:, :, m * chan : (m + 1) * chan].reshape(slots, chan)
        weighted_dep[m] = jnp.dot(rows, precision, precision=HIGHEST, preferred_element_type=F32)
    landed(mod_recv, a2a_recv.at[1])
    model = mod_recv[...].reshape(slots, chan)
    weighted_model = jnp.dot(model, precision, precision=HIGHEST, preferred_element_type=F32)
    answer = jnp.zeros((slots, chan), F32)
    for m in range(MEMBERS):
        misfit = model - dep_recv[:, :, m * chan : (m + 1) * chan].reshape(slots, chan)
        weighted = weighted_model - weighted_dep[m]
        energy = jnp.sum(misfit * weighted, axis=1, keepdims=True) / chan
        answer += weighted / (1.0 + energy)
    ans[...] = answer.reshape(tiles, cap, chan)
    exchange(lambda k: (ans.at[k], lax.rem(me - k + tiles, tiles)), back, 2)
    back[0] = ans[0]
    for copy in cell_copies:
        copy.wait()
    cells_out[0] = cells_in[0]
    cells_out[1] = cells[1]
    cells_out[2] = cells_in[1]
    for q in range(CHUNKS):
        for side in range(2):
            halo_copy(side, q).wait_send()
    landed(dep_recv, a2a_send.at[0])
    landed(mod_recv, a2a_send.at[1])
    for q in range(CHUNKS):
        part = pl.ds(q * nc, nc)
        pltpu.make_async_copy(inc.at[part], inc_out.at[part], out_sem.at[q]).wait()
    landed(back, a2a_recv.at[2])
    forward = [
        remote(back, back_r, geo_send.at[4], geo_recv.at[4], left),
        remote(back, back_l, geo_send.at[5], geo_recv.at[5], right),
    ]
    for copy in forward:
        copy.start()
    landed(back, a2a_send.at[2])
    out = [pltpu.make_async_copy(back, back_out.at[1], back_sem.at[1])]
    out[0].start()
    for copy in forward:
        copy.wait()
    for j, buffer in ((0, back_r), (2, back_l)):
        out.append(pltpu.make_async_copy(buffer, back_out.at[j], back_sem.at[j]))
        out[-1].start()
    for copy in out:
        copy.wait()


def adjoint_kernel(
    chan, cx,
    control, inc_in, back, cells, faces, ocb,
    inc_out, grad_out,
    own, field, grad, inc, inc_sem, own_sem, out_sem,
):
    h = STEPS
    ext = cx + 2 * h
    ny = own.shape[2]
    nc = chan // CHUNKS
    _, tiles, cap, _ = back.shape
    slots = tiles * cap
    own_copy = pltpu.make_async_copy(control, own, own_sem)
    own_copy.start()
    inc_copy = pltpu.make_async_copy(inc_in, inc, inc_sem)
    inc_copy.start()
    eye = lax.broadcasted_iota(I32, (slots, slots), 0) == lax.broadcasted_iota(I32, (slots, slots), 1)
    for j, start, first, count in ((1, h, 0, cx), (0, h + cx, 0, h), (2, 0, cx - h, h)):
        rows_t = back[j].reshape(slots, chan).T
        lhs = jnp.concatenate(split(rows_t), axis=1)
        cell = jnp.sum(jnp.where(eye, cells[j, 0:1], 0), axis=1, keepdims=True)
        for x in range(0, count, 2):
            index = lax.broadcasted_iota(I32, (slots, 2 * ny), 1) + (first + x) * ny
            hot = jnp.where(index == cell, 1.0, 0.0).astype(BF16)
            out = jnp.dot(lhs, jnp.concatenate([hot, hot], axis=0), preferred_element_type=F32)
            field[start + x] = out[:, :ny]
            field[start + x + 1] = out[:, ny:]
    own_copy.wait()
    inc_copy.wait()
    inc_copy = pltpu.make_async_copy(inc, inc_out, inc_sem)
    inc_copy.start()
    own2, grad2 = own.reshape(chan * cx, ny), grad.reshape(chan * cx, ny)
    shift = shifts(ny)

    def out_copy(q):
        part = pl.ds(q * nc, nc)
        return pltpu.make_async_copy(grad.at[part], grad_out.at[part], out_sem.at[q])

    @pl.loop(0, CHUNKS)
    def _(q):
        rows = sweep([field[i, pl.ds(pl.multiple_of(q * nc, nc), nc), :] for i in range(ext)], faces, shift)
        for r in range(cx):
            at = pl.ds(q * nc * cx + r, nc, stride=cx)
            grad2[at, :] = own2[at, :] + jnp.concatenate([ocb[r + h]] * (nc // 8), axis=0) * rows[r]
        out_copy(q).start()

    for q in range(CHUNKS):
        out_copy(q).wait()
    inc_copy.wait()


def body(control, departures, obs_cell, obs_owner, scale_class, sea_mask, class_table, obs_precision):
    fields, levels, cx, ny = control.shape
    chan = fields * levels
    n = obs_cell.shape[0]
    tiles = lax.axis_size("tiles")
    cap = -(-max(2, 2 * n // tiles) // 8) * 8
    slots = tiles * cap
    ext = cx + 2 * STEPS
    flat = control.reshape(chan, cx, ny)
    vmem = pl.BlockSpec(memory_space=pltpu.VMEM)
    smem = pl.BlockSpec(memory_space=pltpu.SMEM)
    hbm = pl.BlockSpec(memory_space=pl.ANY)
    state = jax.ShapeDtypeStruct((chan, cx, ny), F32)
    dma = pltpu.SemaphoreType.DMA
    inc, back, cells, faces, ocb = pl.pallas_call(
        functools.partial(observe_kernel, tiles, cap, chan, cx),
        out_shape=(
            state,
            jax.ShapeDtypeStruct((3, tiles, cap, chan), F32),
            jax.ShapeDtypeStruct((3, 8, slots), I32),
            jax.ShapeDtypeStruct((3, ext, 8, ny), F32),
            jax.ShapeDtypeStruct((ext, 8, ny), F32),
        ),
        in_specs=[smem, hbm] + [vmem] * 6,
        out_specs=(hbm, hbm, vmem, vmem, vmem),
        scratch_shapes=[
            pltpu.VMEM((chan, cx, ny), F32),
            pltpu.VMEM((chan, STEPS, ny), F32),
            pltpu.VMEM((chan, STEPS, ny), F32),
            pltpu.VMEM((chan, cx, ny), F32),
            pltpu.VMEM((2, cx, ny), I32),
            pltpu.VMEM((2, STEPS, ny), I32),
            pltpu.VMEM((2, STEPS, ny), I32),
            pltpu.VMEM((3, 8, slots), I32),
            pltpu.VMEM((2, 8, slots), I32),
            pltpu.VMEM((cx // 2, 2 * ny, slots), BF16),
            pltpu.VMEM((chan, slots), F32),
            pltpu.VMEM((tiles, cap, MEMBERS * chan), F32),
            pltpu.VMEM((tiles, cap, MEMBERS * chan), F32),
            pltpu.VMEM((tiles, cap, chan), F32),
            pltpu.VMEM((tiles, cap, chan), F32),
            pltpu.VMEM((tiles, cap, chan), F32),
            pltpu.VMEM((tiles, cap, chan), F32),
            pltpu.VMEM((tiles, cap, chan), F32),
            pltpu.VMEM((tiles, cap, chan), F32),
            pltpu.VMEM((MEMBERS, slots, chan), F32),
            dma, dma((CHUNKS,)), dma((3,)), dma((2, CHUNKS)), dma((2, CHUNKS)), dma((6,)), dma((6,)), dma((3,)), dma((3,)),
        ],
        compiler_params=pltpu.CompilerParams(
            collective_id=0, has_side_effects=True, vmem_limit_bytes=63 * 2**20
        ),
        name="observe",
    )(class_table, flat, departures, obs_cell.reshape(1, n), obs_owner.reshape(1, n), scale_class, sea_mask, obs_precision)
    increment, gradient = pl.pallas_call(
        functools.partial(adjoint_kernel, chan, cx),
        out_shape=(state, state),
        in_specs=[hbm, hbm] + [vmem] * 4,
        out_specs=(hbm, hbm),
        scratch_shapes=[
            pltpu.VMEM((chan, cx, ny), F32),
            pltpu.VMEM((ext, chan, ny), F32),
            pltpu.VMEM((chan, cx, ny), F32),
            pltpu.VMEM((chan, cx, ny), F32),
            dma, dma, dma((CHUNKS,)),
        ],
        compiler_params=pltpu.CompilerParams(vmem_limit_bytes=63 * 2**20),
        name="adjoint",
    )(flat, inc, back, cells, faces, ocb)
    return increment.reshape(control.shape), gradient.reshape(control.shape)


def solution(mesh):
    return jax.shard_map(
        body,
        mesh=mesh,
        in_specs=(
            P("groups", None, "tiles", None),
            P(("groups", "tiles"), None),
            P(("groups", "tiles")),
            P(("groups", "tiles"), None),
            P("tiles", None),
            P("tiles", None),
            P(),
            P("tiles", None),
        ),
        out_specs=(P("groups", None, "tiles", None), P("groups", None, "tiles", None)),
        check_vma=False,
    )
```
